32 devices in a mesh: groups: 2 (over y), store: 16 (over z, x, core).
Axes of the slice: x: 2, y: 2, z: 4, core: 2. Of those that a mesh axis runs over, the one named last changes fastest.
Arguments:
- tokens: bfloat16 [32768, 8192], P('groups', 'store'), parts along dimension 0, may hold values from -6 to 6
- up_grad: bfloat16 [32768, 28672], P('groups', 'store'), parts along dimension 0, may hold values from -6 to 6
- in_index: int32 [8, 32], replicated, may hold values from 0 to 255
- in_values: bfloat16 [8, 32, 32, 8], replicated, may hold values from -0.1875 to 0.1875
- out_index: int32 [8, 112], replicated, may hold values from 0 to 895
- out_values: bfloat16 [8, 112, 32, 8], replicated, may hold values from -0.09375 to 0.09375
- stored: bfloat16 [8192, 4096], P(('groups', 'store')), parts along dimension 0, may hold values from -6 to 6
Outputs:
- scores: float32 [8, 4096], P('groups', 'store'), parts along dimension 0
The draws below stay inside these ranges and needn't reach their ends.
There are 2 independent parts, one for each index of `groups`. The reference program is written for one: setup_inputs(seed, part) draws one part's arguments, and reference() takes and returns one part's arrays. A program takes and returns all parts, laid end to end along the dimension named above; an argument that names none is the same for every part. Nothing has to cross between parts.
All inputs are finite; a program needn't handle non-finite values.
Results may differ from the reference program's by a relative error of at most 0.0034.
Values sent between devices are 32-bit elements; how exact they have to be, the bound alone decides.
No kernel may reach another device: no remote copies, remote signals or barrier semaphores. Data moves between devices by JAX's collectives and lax.ppermute only.
A program may use at most 192 MiB of HBM per device.

```python
import jax
import jax.numpy as jnp
from jax import lax

D = 8192
FF = 28672
SEQS = 4
LEN = 4096
BLOCK = 32
CGROUPS = 8
CWIDTH = 8
K_IN = 32
K_OUT = 112
PROJ = 64
TOKENS = 16384
NB_IN = 256
NB_OUT = 896
ROWS = 4096


def with_ends(array, stream_key, smallest, high):
    place = [jax.random.randint(jax.random.fold_in(stream_key, axis), (), 0, length) for axis, length in enumerate(array.shape)]
    widest = array.shape.index(max(array.shape))
    next_to = place[:widest] + [(place[widest] + 1) % array.shape[widest]] + place[widest + 1:]
    return array.at[tuple(place)].set(smallest).at[tuple(next_to)].set(high)


def level_of(rng, shape, split, smallest, high):
    def one(axis_at, blocks):
        heights = jax.random.uniform(jax.random.fold_in(jax.random.fold_in(rng, 6), axis_at), (blocks,), jnp.float32, smallest / len(split), high / len(split))
        return jnp.repeat(jnp.exp(heights), shape[axis_at] // blocks).reshape((-1,) + (1,) * (len(shape) - axis_at - 1))

    loudness = one(*split[0])
    for cut in split[1:]:
        loudness = loudness * one(*cut)
    return loudness


def noise(rng, shape, deviation, limit, shards=(), held_as=jnp.bfloat16):
    gain = level_of(rng, shape, shards, -0.22, 0.18) if shards else 1.0
    values = jax.random.normal(rng, shape, jnp.float32) * deviation * gain
    return jnp.minimum(jnp.maximum(values, -limit), limit).astype(held_as)


def setup_inputs(seed: int = 0, part: int = 0) -> dict:
    splits = jax.random.split(jax.random.key(seed), 8)
    own_keys = jax.random.split(jax.random.fold_in(splits[7], part), 8)
    tokens = noise(own_keys[0], (TOKENS, D), 1.0, 6.0, ((1, 16),))
    up_grad = noise(own_keys[1], (TOKENS, FF), 1.0, 6.0, ((1, 16),))
    in_index = with_ends(jax.random.randint(splits[2], (CGROUPS, K_IN), 0, NB_IN), jax.random.fold_in(splits[2], 1), 0, NB_IN - 1).astype(jnp.int32)
    in_values = noise(splits[3], (CGROUPS, K_IN, BLOCK, CWIDTH), (K_IN * BLOCK) ** -0.5, 0.1875)
    out_index = with_ends(jax.random.randint(splits[4], (CGROUPS, K_OUT), 0, NB_OUT), jax.random.fold_in(splits[4], 1), 0, NB_OUT - 1).astype(jnp.int32)
    out_values = noise(splits[5], (CGROUPS, K_OUT, BLOCK, CWIDTH), (K_OUT * BLOCK) ** -0.5, 0.09375)
    stored = noise(own_keys[6], (ROWS, PROJ * PROJ), 1.0, 6.0, ((0, 16),))
    return {"tokens": tokens, "up_grad": up_grad, "in_index": in_index, "in_values": in_values, "out_index": out_index, "out_values": out_values, "stored": stored}


def dense_projection(index, values, count):
    onehot = (index[:, :, None] == jnp.arange(count, dtype=jnp.int32)[None, None, :]).astype(jnp.float32)
    dense = jnp.einsum("ckn,ckrw->nrcw", onehot, values.astype(jnp.float32))
    return dense.reshape(count * values.shape[2], values.shape[0] * values.shape[3]).astype(jnp.bfloat16)


def reference(tokens, up_grad, in_index, in_values, out_index, out_values, stored):
    in_proj = dense_projection(in_index, in_values, NB_IN)
    out_proj = dense_projection(out_index, out_values, NB_OUT)
    inputs = jnp.dot(tokens, in_proj, preferred_element_type=jnp.float32)
    outputs = jnp.dot(up_grad, out_proj, preferred_element_type=jnp.float32)
    left = inputs.reshape(SEQS, LEN, PROJ)
    right = outputs.reshape(SEQS, LEN, PROJ)
    example = jnp.einsum("slp,slq->spq", left, right, precision=lax.Precision.HIGHEST) / LEN
    example_grad = example.reshape(SEQS, PROJ * PROJ).astype(jnp.bfloat16)
    return jnp.dot(example_grad, stored.T, preferred_element_type=jnp.float32)
```

```python
import functools

import jax
import jax.numpy as jnp
from jax import lax
from jax.experimental import pallas as pl
from jax.experimental.pallas import tpu as pltpu
from jax.sharding import PartitionSpec as P

LEN = 4096
BLOCK = 32
LANES = 128
HALF = LANES // 2
SLOTS = 4
VMEM_LIMIT = 16 * 1024 * 1024

ANY = pl.BlockSpec(memory_space=pl.ANY)
IN_HBM = pl.BlockSpec(memory_space=pltpu.HBM)
IN_VMEM = pl.BlockSpec(memory_space=pltpu.VMEM)
IN_SMEM = pl.BlockSpec(memory_space=pltpu.SMEM)
PARAMS = pltpu.CompilerParams(vmem_limit_bytes=VMEM_LIMIT)


def build_in(first, index_ref, values_ref, w_ref, list_ref, acc_ref):
    groups, picks = index_ref.shape
    cwidth = values_ref.shape[1]
    count = acc_ref.shape[0]
    acc_ref[...] = jnp.zeros_like(acc_ref)
    found = jnp.int32(0)
    for c in range(groups):

        def scan(k, found, c=c):
            block = index_ref[c, k] - first
            list_ref[0, found] = c * picks + k
            list_ref[1, found] = block
            list_ref[2, found] = c * cwidth
            return found + jnp.where((block >= 0) & (block < count), 1, 0).astype(jnp.int32)

        found = lax.fori_loop(0, picks, scan, found, unroll=8)

    def add(i, carry):
        rows = pl.ds(pl.multiple_of(list_ref[2, i], cwidth), cwidth)
        acc_ref[list_ref[1, i], rows, :BLOCK] += values_ref[list_ref[0, i]].astype(jnp.float32)
        return carry

    lax.fori_loop(0, found, add, jnp.int32(0))
    for n in range(count):
        block = acc_ref[n]
        wide = jnp.concatenate([block, jnp.zeros_like(block)], axis=0).T[:BLOCK]
        rows = slice(n * BLOCK, (n + 1) * BLOCK)
        w_ref[0, rows] = wide.astype(jnp.bfloat16)
        w_ref[1, rows] = pltpu.roll(wide, HALF, 1).astype(jnp.bfloat16)


def build_out_kernel(count, first_ref, index_ref, values_ref, *rest):
    w_ref, by_block_ref, wide_ref = rest[-3:]
    groups, picks = index_ref.shape
    cwidth = values_ref.shape[1] // BLOCK
    ids = lax.broadcasted_iota(jnp.int32, (LANES, picks), 0) + first_ref[0]
    for c in range(groups):
        chosen = (index_ref[c : c + 1, :] == ids).astype(jnp.float32).astype(jnp.bfloat16)
        by_block_ref[c] = lax.dot_general(
            values_ref[c], chosen, (((1,), (1,)), ((), ())), preferred_element_type=jnp.float32
        )
    low = lax.broadcasted_iota(jnp.int32, (count, LANES), 1) < HALF
    for r in range(0, BLOCK, 2):
        rows = [
            by_block_ref[c, (r + odd) * cwidth : (r + odd + 1) * cwidth, :]
            for odd in (0, 1)
            for c in range(groups)
        ]
        pair = jnp.concatenate(rows, axis=0).T[:count]
        swapped = pltpu.roll(pair, HALF, 1)
        wide_ref[0, pl.ds(r, count, stride=BLOCK), :] = jnp.where(low, pair, 0.0)
        wide_ref[0, pl.ds(r + 1, count, stride=BLOCK), :] = jnp.where(low, swapped, 0.0)
        wide_ref[1, pl.ds(r, count, stride=BLOCK), :] = jnp.where(low, 0.0, swapped)
        wide_ref[1, pl.ds(r + 1, count, stride=BLOCK), :] = jnp.where(low, 0.0, pair)
    w_ref[...] = wide_ref[...].astype(jnp.bfloat16)


def build_out(index, values, first, count, after=()):
    groups, picks = index.shape
    values = values.transpose(0, 2, 3, 1).reshape(groups, -1, picks)
    rows = count * BLOCK
    return pl.pallas_call(
        functools.partial(build_out_kernel, count),
        out_shape=pltpu.VMEM((2, rows, LANES), jnp.bfloat16),
        in_specs=[IN_SMEM, IN_VMEM, IN_VMEM] + [ANY] * len(after),
        out_specs=IN_VMEM,
        scratch_shapes=[
            pltpu.VMEM((groups, values.shape[1], LANES), jnp.float32),
            pltpu.VMEM((2, rows, LANES), jnp.float32),
        ],
        compiler_params=PARAMS,
        cost_estimate=pl.CostEstimate(flops=10**9, bytes_accessed=values.size * 2, transcendentals=0),
    )(first[None].astype(jnp.int32), index, values, *after)


def project_kernel(tile, cuts, has_add, builds, after, *refs):
    refs = list(refs)
    roles_ref = refs.pop(0)
    x_hbm = refs.pop(0)
    if builds:
        index_hbm, values_hbm = refs.pop(0), refs.pop(0)
    else:
        w_ref = refs.pop(0)
    add_ref = refs.pop(0) if has_add else None
    refs = refs[after:]
    outs = [refs.pop(0) for _ in range(1 + max(cut[0] for cut in cuts))]
    if builds:
        w_ref = refs.pop(0)
    buf, sems = refs.pop(0), refs.pop(0)
    steps, filled = [], [0] * len(outs)
    for array, role, start, rows in cuts:
        for at in range(0, rows, tile):
            steps.append((array, role, start + at, filled[array]))
            filled[array] += tile

    def copies(i):
        _, role, row, _ = steps[i]
        base = pl.multiple_of(roles_ref[role] * LEN + roles_ref[4] * (LEN // 4) + row, tile)
        slot = i % SLOTS
        return [
            pltpu.make_async_copy(
                x_hbm.at[pl.ds(base + side * (LEN // 2), tile), :], buf.at[slot, side], sems.at[slot, side]
            )
            for side in (0, 1)
        ]

    if builds:
        index_ref, values_ref, build_sems, list_ref, acc_ref = refs
        loads = [
            pltpu.make_async_copy(index_hbm, index_ref, build_sems.at[0]),
            pltpu.make_async_copy(values_hbm, values_ref, build_sems.at[1]),
        ]
        for load in loads:
            load.start()
    for i in range(min(SLOTS, len(steps))):
        for copy in copies(i):
            copy.start()
    if builds:
        for load in loads:
            load.wait()
        build_in(roles_ref[5], index_ref, values_ref, w_ref, list_ref, acc_ref)
    for i, (array, _, _, at) in enumerate(steps):
        for copy in copies(i):
            copy.wait()
        slot = i % SLOTS
        value = jnp.dot(buf[slot, 0], w_ref[0], preferred_element_type=jnp.float32)
        value += jnp.dot(buf[slot, 1], w_ref[1], preferred_element_type=jnp.float32)
        if has_add:
            value += add_ref[i * tile : (i + 1) * tile, :]
        outs[array][at : at + tile, :] = value
        if i + SLOTS < len(steps):
            for copy in copies(i + SLOTS):
                copy.start()


def project(x, w, roles, add, tile, cuts, after=()):
    depth = x.shape[1]
    x = pltpu.with_memory_space_constraint(x, pltpu.HBM)
    rows = sum(cut[3] for cut in cuts)
    builds = isinstance(w, tuple)
    out_shape = [
        pltpu.VMEM((sum(cut[3] for cut in cuts if cut[0] == array), LANES), jnp.float32)
        for array in range(1 + max(cut[0] for cut in cuts))
    ]
    scratch = [
        pltpu.VMEM((SLOTS, 2, tile, depth), x.dtype),
        pltpu.SemaphoreType.DMA((SLOTS, 2)),
    ]
    if builds:
        index, values, count = w
        groups, picks = index.shape
        cwidth = values.shape[3]
        values = values.transpose(0, 1, 3, 2).reshape(groups * picks, cwidth, BLOCK)
        args = [roles, x, index, values]
        in_specs = [IN_SMEM, IN_HBM, IN_HBM, IN_HBM]
        out_shape.append(pltpu.VMEM((2, count * BLOCK, LANES), jnp.bfloat16))
        scratch += [
            pltpu.SMEM(index.shape, index.dtype),
            pltpu.VMEM(values.shape, values.dtype),
            pltpu.SemaphoreType.DMA((2,)),
            pltpu.SMEM((3, groups * picks), jnp.int32),
            pltpu.VMEM((count, groups * cwidth, LANES), jnp.float32),
        ]
    else:
        args = [roles, x, w]
        in_specs = [IN_SMEM, IN_HBM, IN_VMEM]
    if add is not None:
        args.append(add)
        in_specs.append(IN_VMEM)
    return pl.pallas_call(
        functools.partial(project_kernel, tile, cuts, add is not None, builds, len(after)),
        out_shape=out_shape,
        in_specs=in_specs + [ANY] * len(after),
        out_specs=[IN_VMEM] * len(out_shape),
        scratch_shapes=scratch,
        compiler_params=PARAMS,
        cost_estimate=pl.CostEstimate(
            flops=rows * depth * LANES, bytes_accessed=rows * depth, transcendentals=0
        ),
    )(*args, *after)


def contract(left, right):
    pair = lax.dot_general(
        left,
        right,
        (((0,), (0,)), ((), ())),
        precision=lax.Precision.HIGHEST,
        preferred_element_type=jnp.float32,
    )
    return pair[:HALF, :HALF] + pair[HALF:, HALF:]


def reduced_examples(tokens, up_grad, in_index, in_values, out_index, out_values):
    rank = lax.axis_index("store")
    core, x, z_low = rank % 2, (rank // 2) % 2, (rank // 4) % 2

    def swap(value, bit):
        return lax.ppermute(value, "store", [(i, i ^ bit) for i in range(16)])

    feat_blocks = tokens.shape[1] // BLOCK
    hidden_blocks = up_grad.shape[1] // BLOCK

    def roles(half):
        seqs = [1 - x, x, 3 - x, 2 + x]
        return jnp.stack([*seqs, half, rank * feat_blocks]).astype(jnp.int32)

    send, keep = roles(1 - core), roles(core)
    rows = LEN // 4
    half = rows // 2
    in_tile, out_tile = 256, 256

    def z_halves(value):
        halves = value.reshape(2, half, LANES)
        gone = lax.dynamic_index_in_dim(halves, 1 - z_low, 0, keepdims=False)
        kept = lax.dynamic_index_in_dim(halves, z_low, 0, keepdims=False)
        return kept + swap(gone, 4)

    def z_whole(kept):
        got = swap(kept, 4)
        return jnp.where(z_low == 0, jnp.stack([kept, got]), jnp.stack([got, kept])).reshape(-1, LANES)

    whole_a = [(0, 0, 0, rows), (1, 1, 0, rows)]
    whole_b = [(0, 2, 0, rows), (1, 3, 0, rows)]
    sent, in_w = project(
        tokens,
        (in_index, in_values, feat_blocks),
        send,
        None,
        in_tile,
        [(0, s, 0, rows) for s in range(4)],
    )
    got = swap(sent, 1)
    out_w = build_out(out_index, out_values, rank * hidden_blocks, hidden_blocks, after=(sent,))
    oa, ma, ob, mb = project(
        tokens, in_w, keep, got, in_tile, [(s, s, 0, rows) for s in range(4)], after=(out_w,)
    )
    in_a = ma + swap(oa, 2)
    in_b = mb + swap(ob, 2)
    (sent,) = project(
        up_grad, out_w, send, None, out_tile, [(0, 2, 0, rows), (0, 3, 0, rows)], after=(mb,)
    )
    got_b = swap(sent, 1)
    (sent,) = project(
        up_grad, out_w, send, None, out_tile, [(0, 0, 0, rows), (0, 1, 0, rows)], after=(in_a, sent)
    )
    got_a = swap(sent, 1)
    in_a = z_halves(in_a)
    ob, mb = project(up_grad, out_w, keep, got_b, out_tile, whole_b, after=(in_a, sent))
    in_a = in_a + swap(in_a, 8)
    in_b = z_halves(in_b)
    oa, ma = project(up_grad, out_w, keep, got_a, out_tile, whole_a, after=(mb, in_a))
    in_a = z_whole(in_a)
    out_b = z_halves(mb + swap(ob, 2))
    in_b = in_b + swap(in_b, 8)
    out_a = ma + swap(oa, 2)
    example = jnp.stack([contract(in_a, out_a), contract(in_b, out_b)]).reshape(-1, LANES)
    for bit in (1, 4, 8):
        example = example + swap(example, bit)
    other = swap(example, 2)
    example, other = example.reshape(2, HALF * HALF), other.reshape(2, HALF * HALF)
    first = jnp.where(x == 0, example, other)
    second = jnp.where(x == 0, other, example)
    return jnp.stack([first, second], axis=1).reshape(4, HALF * HALF) / LEN


def summed_examples(tokens, up_grad, in_index, in_values, out_index, out_values):
    rank = lax.axis_index("store")
    seqs = tokens.shape[0] // LEN
    feat_blocks = tokens.shape[1] // BLOCK
    hidden_blocks = up_grad.shape[1] // BLOCK
    out_proj = build_out(out_index, out_values, rank * hidden_blocks, hidden_blocks)
    rows = LEN // 4

    def packed(kind, w):
        made = []
        for s in range(0, seqs, 2):
            for h in (0, 1):
                roles = jnp.stack([s, s + 1, s, s, h, rank * feat_blocks]).astype(jnp.int32)
                first, second, *rest = project(
                    kind, w, roles, None, 256, [(0, 0, 0, rows), (1, 1, 0, rows)]
                )
                if rest:
                    w = rest[0]
                made.append(jnp.stack([first, second]))
        return jnp.concatenate(made)

    ins, outs = lax.psum(
        (packed(tokens, (in_index, in_values, feat_blocks)), packed(up_grad, out_proj)), "store"
    )
    pair = jnp.einsum("slp,slq->spq", ins, outs, precision=lax.Precision.HIGHEST)
    pair = pair[:, :HALF, :HALF] + pair[:, HALF:, HALF:]
    pair = pair.reshape(seqs // 2, 2, 2, HALF * HALF).sum(1) / LEN
    return pair.reshape(seqs, HALF * HALF)


def on_device(size, tokens, up_grad, in_index, in_values, out_index, out_values, stored):
    whole = reduced_examples if size == 16 and tokens.shape[0] == 4 * LEN else summed_examples
    example = whole(tokens, up_grad, in_index, in_values, out_index, out_values)
    return lax.dot_general(
        example.astype(jnp.bfloat16),
        stored,
        (((1,), (1,)), ((), ())),
        preferred_element_type=jnp.float32,
    )


def solution(mesh):
    return jax.shard_map(
        functools.partial(on_device, mesh.shape["store"]),
        mesh=mesh,
        in_specs=(
            P("groups", "store"),
            P("groups", "store"),
            P(),
            P(),
            P(),
            P(),
            P(("groups", "store"), None),
        ),
        out_specs=P("groups", "store"),
        check_vma=False,
    )
```

```python
import functools

import jax
import jax.numpy as jnp
from jax import lax
from jax.experimental import pallas as pl
from jax.experimental.pallas import tpu as pltpu
from jax.sharding import PartitionSpec as P

LEN = 4096
BLOCK = 32
LANES = 128
HALF = LANES // 2
SLOTS = 4
VMEM_LIMIT = 16 * 1024 * 1024

ANY = pl.BlockSpec(memory_space=pl.ANY)
IN_HBM = pl.BlockSpec(memory_space=pltpu.HBM)
IN_VMEM = pl.BlockSpec(memory_space=pltpu.VMEM)
IN_SMEM = pl.BlockSpec(memory_space=pltpu.SMEM)
PARAMS = pltpu.CompilerParams(vmem_limit_bytes=VMEM_LIMIT)


def build_in(first, index_ref, values_ref, w_ref, list_ref, acc_ref):
    groups, picks = index_ref.shape
    cwidth = values_ref.shape[1]
    count = acc_ref.shape[0]
    acc_ref[...] = jnp.zeros_like(acc_ref)
    found = jnp.int32(0)
    for c in range(groups):

        def scan(k, found, c=c):
            block = index_ref[c, k] - first
            list_ref[0, found] = c * picks + k
            list_ref[1, found] = block
            list_ref[2, found] = c * cwidth
            return found + jnp.where((block >= 0) & (block < count), 1, 0).astype(jnp.int32)

        found = lax.fori_loop(0, picks, scan, found, unroll=8)

    def add(i, carry):
        rows = pl.ds(pl.multiple_of(list_ref[2, i], cwidth), cwidth)
        acc_ref[list_ref[1, i], rows, :BLOCK] += values_ref[list_ref[0, i]].astype(jnp.float32)
        return carry

    lax.fori_loop(0, found, add, jnp.int32(0))
    for n in range(count):
        block = acc_ref[n]
        wide = jnp.concatenate([block, jnp.zeros_like(block)], axis=0).T[:BLOCK]
        rows = slice(n * BLOCK, (n + 1) * BLOCK)
        w_ref[0, rows] = wide.astype(jnp.bfloat16)
        w_ref[1, rows] = pltpu.roll(wide, HALF, 1).astype(jnp.bfloat16)


def build_out_kernel(count, first_ref, index_ref, values_ref, *rest):
    w_ref, by_block_ref, wide_ref = rest[-3:]
    groups, picks = index_ref.shape
    cwidth = values_ref.shape[1] // BLOCK
    ids = lax.broadcasted_iota(jnp.int32, (LANES, picks), 0) + first_ref[0]
    for c in range(groups):
        chosen = (index_ref[c : c + 1, :] == ids).astype(jnp.float32).astype(jnp.bfloat16)
        by_block_ref[c] = lax.dot_general(
            values_ref[c], chosen, (((1,), (1,)), ((), ())), preferred_element_type=jnp.float32
        )
    low = lax.broadcasted_iota(jnp.int32, (count, LANES), 1) < HALF
    for r in range(0, BLOCK, 2):
        rows = [
            by_block_ref[c, (r + odd) * cwidth : (r + odd + 1) * cwidth, :]
            for odd in (0, 1)
            for c in range(groups)
        ]
        pair = jnp.concatenate(rows, axis=0).T[:count]
        swapped = pltpu.roll(pair, HALF, 1)
        wide_ref[0, pl.ds(r, count, stride=BLOCK), :] = jnp.where(low, pair, 0.0)
        wide_ref[0, pl.ds(r + 1, count, stride=BLOCK), :] = jnp.where(low, swapped, 0.0)
        wide_ref[1, pl.ds(r, count, stride=BLOCK), :] = jnp.where(low, 0.0, swapped)
        wide_ref[1, pl.ds(r + 1, count, stride=BLOCK), :] = jnp.where(low, 0.0, pair)
    w_ref[...] = wide_ref[...].astype(jnp.bfloat16)


def build_out(index, values, first, count, after=()):
    groups, picks = index.shape
    values = values.transpose(0, 2, 3, 1).reshape(groups, -1, picks)
    rows = count * BLOCK
    return pl.pallas_call(
        functools.partial(build_out_kernel, count),
        out_shape=pltpu.VMEM((2, rows, LANES), jnp.bfloat16),
        in_specs=[IN_SMEM, IN_VMEM, IN_VMEM] + [ANY] * len(after),
        out_specs=IN_VMEM,
        scratch_shapes=[
            pltpu.VMEM((groups, values.shape[1], LANES), jnp.float32),
            pltpu.VMEM((2, rows, LANES), jnp.float32),
        ],
        compiler_params=PARAMS,
        cost_estimate=pl.CostEstimate(flops=10**9, bytes_accessed=values.size * 2, transcendentals=0),
    )(first[None].astype(jnp.int32), index, values, *after)


def project_kernel(tile, cuts, has_add, builds, after, through, *refs):
    refs = list(refs)
    roles_ref = refs.pop(0)
    x_hbm = refs.pop(0)
    if builds:
        index_hbm, values_hbm = refs.pop(0), refs.pop(0)
    else:
        w_ref = refs.pop(0)
    add_ref = refs.pop(0) if has_add else None
    refs = refs[after + through :]
    outs = [refs.pop(0) for _ in range(1 + max(cut[0] for cut in cuts))]
    if builds:
        w_ref = refs.pop(0)
    refs = refs[through:]
    buf, sems = refs.pop(0), refs.pop(0)
    steps, filled = [], [0] * len(outs)
    for array, role, start, rows in cuts:
        for at in range(0, rows, tile):
            steps.append((array, role, start + at, filled[array]))
            filled[array] += tile

    def copies(i):
        _, role, row, _ = steps[i]
        base = pl.multiple_of(roles_ref[role] * LEN + roles_ref[4] * (LEN // 4) + row, tile)
        slot = i % SLOTS
        return [
            pltpu.make_async_copy(
                x_hbm.at[pl.ds(base + side * (LEN // 2), tile), :], buf.at[slot, side], sems.at[slot, side]
            )
            for side in (0, 1)
        ]

    if builds:
        index_ref, values_ref, build_sems, list_ref, acc_ref = refs
        loads = [
            pltpu.make_async_copy(index_hbm, index_ref, build_sems.at[0]),
            pltpu.make_async_copy(values_hbm, values_ref, build_sems.at[1]),
        ]
        for load in loads:
            load.start()
    for i in range(min(SLOTS, len(steps))):
        for copy in copies(i):
            copy.start()
    if builds:
        for load in loads:
            load.wait()
        build_in(roles_ref[5], index_ref, values_ref, w_ref, list_ref, acc_ref)
    for i, (array, _, _, at) in enumerate(steps):
        for copy in copies(i):
            copy.wait()
        slot = i % SLOTS
        value = jnp.dot(buf[slot, 0], w_ref[0], preferred_element_type=jnp.float32)
        value += jnp.dot(buf[slot, 1], w_ref[1], preferred_element_type=jnp.float32)
        if has_add:
            value += add_ref[i * tile : (i + 1) * tile, :]
        outs[array][at : at + tile, :] = value
        if i + SLOTS < len(steps):
            for copy in copies(i + SLOTS):
                copy.start()


def project(x, w, roles, add, tile, cuts, after=(), through=()):
    depth = x.shape[1]
    x = pltpu.with_memory_space_constraint(x, pltpu.HBM)
    rows = sum(cut[3] for cut in cuts)
    builds = isinstance(w, tuple)
    out_shape = [
        pltpu.VMEM((sum(cut[3] for cut in cuts if cut[0] == array), LANES), jnp.float32)
        for array in range(1 + max(cut[0] for cut in cuts))
    ]
    scratch = [
        pltpu.VMEM((SLOTS, 2, tile, depth), x.dtype),
        pltpu.SemaphoreType.DMA((SLOTS, 2)),
    ]
    if builds:
        index, values, count = w
        groups, picks = index.shape
        cwidth = values.shape[3]
        values = values.transpose(0, 1, 3, 2).reshape(groups * picks, cwidth, BLOCK)
        index = pltpu.with_memory_space_constraint(index, pltpu.HBM)
        values = pltpu.with_memory_space_constraint(values, pltpu.HBM)
        args = [roles, x, index, values]
        in_specs = [IN_SMEM, IN_HBM, IN_HBM, IN_HBM]
        out_shape.append(pltpu.VMEM((2, count * BLOCK, LANES), jnp.bfloat16))
        scratch += [
            pltpu.SMEM(index.shape, index.dtype),
            pltpu.VMEM(values.shape, values.dtype),
            pltpu.SemaphoreType.DMA((2,)),
            pltpu.SMEM((3, groups * picks), jnp.int32),
            pltpu.VMEM((count, groups * cwidth, LANES), jnp.float32),
        ]
    else:
        args = [roles, x, w]
        in_specs = [IN_SMEM, IN_HBM, IN_VMEM]
    if add is not None:
        args.append(add)
        in_specs.append(IN_VMEM)
    return pl.pallas_call(
        functools.partial(project_kernel, tile, cuts, add is not None, builds, len(after), len(through)),
        out_shape=out_shape + [jax.ShapeDtypeStruct(t.shape, t.dtype) for t in through],
        in_specs=in_specs + [ANY] * (len(after) + len(through)),
        out_specs=[IN_VMEM] * len(out_shape) + [ANY] * len(through),
        input_output_aliases={
            len(args) + len(after) + i: len(out_shape) + i for i in range(len(through))
        },
        scratch_shapes=scratch,
        compiler_params=PARAMS,
        cost_estimate=pl.CostEstimate(
            flops=rows * depth * LANES, bytes_accessed=rows * depth, transcendentals=0
        ),
    )(*args, *after, *through)


def held(values, after):
    count = len(values)
    return pl.pallas_call(
        lambda *refs: None,
        out_shape=[jax.ShapeDtypeStruct(v.shape, v.dtype) for v in values],
        in_specs=[ANY] * (count + len(after)),
        out_specs=[ANY] * count,
        input_output_aliases={i: i for i in range(count)},
        cost_estimate=pl.CostEstimate(flops=0, bytes_accessed=0, transcendentals=0),
    )(*values, *after)


def contract(left, right):
    pair = lax.dot_general(
        left,
        right,
        (((0,), (0,)), ((), ())),
        precision=lax.Precision.HIGHEST,
        preferred_element_type=jnp.float32,
    )
    return pair[:HALF, :HALF] + pair[HALF:, HALF:]


def reduced_examples(tokens, up_grad, in_index, in_values, out_index, out_values):
    rank = lax.axis_index("store")
    core, x, z_low = rank % 2, (rank // 2) % 2, (rank // 4) % 2

    def swap(value, bit):
        return lax.ppermute(value, "store", [(i, i ^ bit) for i in range(16)])

    feat_blocks = tokens.shape[1] // BLOCK
    hidden_blocks = up_grad.shape[1] // BLOCK

    def roles(half):
        seqs = [1 - x, x, 3 - x, 2 + x]
        return jnp.stack([*seqs, half, rank * feat_blocks]).astype(jnp.int32)

    send, keep = roles(1 - core), roles(core)
    rows = LEN // 4
    half = rows // 2
    in_tile, out_tile = 256, 256

    def z_halves(value):
        halves = value.reshape(2, half, LANES)
        gone = lax.dynamic_index_in_dim(halves, 1 - z_low, 0, keepdims=False)
        kept = lax.dynamic_index_in_dim(halves, z_low, 0, keepdims=False)
        return kept, swap(gone, 4)

    def z_whole(kept):
        got = swap(kept, 4)
        return jnp.where(z_low == 0, jnp.stack([kept, got]), jnp.stack([got, kept])).reshape(-1, LANES)

    whole_a = [(0, 0, 0, rows), (1, 1, 0, rows)]
    whole_b = [(0, 2, 0, rows), (1, 3, 0, rows)]
    sent, in_w = project(
        tokens,
        (in_index, in_values, feat_blocks),
        send,
        None,
        in_tile,
        [(0, s, 0, rows) for s in range(4)],
    )
    got = swap(sent, 1)
    out_w = build_out(out_index, out_values, rank * hidden_blocks, hidden_blocks, after=(sent,))
    oa, in_a, ob, in_b = project(
        tokens, in_w, keep, got, in_tile, [(s, s, 0, rows) for s in range(4)], after=(out_w,)
    )
    got_in_a, got_in_b = swap(oa, 2), swap(ob, 2)
    sent_b, sent_a, in_a = project(
        up_grad,
        out_w,
        send,
        None,
        out_tile,
        [(0, 2, 0, rows), (0, 3, 0, rows), (1, 0, 0, rows), (1, 1, 0, rows)],
        after=(in_b,),
        through=(in_a,),
    )
    in_a = in_a + got_in_a
    sent_b, sent_a = held((sent_b, sent_a), (in_a,))
    got_b, got_a = swap(sent_b, 1), swap(sent_a, 1)
    in_a, got_in_a = z_halves(in_a)
    ob, out_b, in_a, in_b = project(
        up_grad, out_w, keep, got_b, out_tile, whole_b, after=(sent_a,), through=(in_a, in_b)
    )
    got_out_b = swap(ob, 2)
    in_a = in_a + got_in_a
    got_in_a = swap(in_a, 8)
    in_b, got_z_b = z_halves(in_b + got_in_b)
    oa, out_a, out_b, in_b = project(
        up_grad, out_w, keep, got_a, out_tile, whole_a, after=(in_a,), through=(out_b, in_b)
    )
    in_b = in_b + got_z_b
    (in_a,) = held((in_a + got_in_a,), (oa,))
    (oa,) = held((oa,), (in_b,))
    got_out_a = swap(oa, 2)
    in_a = z_whole(in_a)
    in_b = in_b + swap(in_b, 8)
    out_b, got_out_b = z_halves(out_b + got_out_b)
    out_b = out_b + got_out_b
    out_a = out_a + got_out_a
    example = jnp.stack([contract(in_a, out_a), contract(in_b, out_b)]).reshape(-1, LANES)
    for bit in (1, 4, 8):
        example = example + swap(example, bit)
    other = swap(example, 2)
    example, other = example.reshape(2, HALF * HALF), other.reshape(2, HALF * HALF)
    first = jnp.where(x == 0, example, other)
    second = jnp.where(x == 0, other, example)
    return jnp.stack([first, second], axis=1).reshape(4, HALF * HALF) / LEN


def summed_examples(tokens, up_grad, in_index, in_values, out_index, out_values):
    rank = lax.axis_index("store")
    seqs = tokens.shape[0] // LEN
    feat_blocks = tokens.shape[1] // BLOCK
    hidden_blocks = up_grad.shape[1] // BLOCK
    out_proj = build_out(out_index, out_values, rank * hidden_blocks, hidden_blocks)
    rows = LEN // 4

    def packed(kind, w):
        made = []
        for s in range(0, seqs, 2):
            for h in (0, 1):
                roles = jnp.stack([s, s + 1, s, s, h, rank * feat_blocks]).astype(jnp.int32)
                first, second, *rest = project(
                    kind, w, roles, None, 256, [(0, 0, 0, rows), (1, 1, 0, rows)]
                )
                if rest:
                    w = rest[0]
                made.append(jnp.stack([first, second]))
        return jnp.concatenate(made)

    ins, outs = lax.psum(
        (packed(tokens, (in_index, in_values, feat_blocks)), packed(up_grad, out_proj)), "store"
    )
    pair = jnp.einsum("slp,slq->spq", ins, outs, precision=lax.Precision.HIGHEST)
    pair = pair[:, :HALF, :HALF] + pair[:, HALF:, HALF:]
    pair = pair.reshape(seqs // 2, 2, 2, HALF * HALF).sum(1) / LEN
    return pair.reshape(seqs, HALF * HALF)


def on_device(size, tokens, up_grad, in_index, in_values, out_index, out_values, stored):
    whole = reduced_examples if size == 16 and tokens.shape[0] == 4 * LEN else summed_examples
    example = whole(tokens, up_grad, in_index, in_values, out_index, out_values)
    return lax.dot_general(
        example.astype(jnp.bfloat16),
        stored,
        (((1,), (1,)), ((), ())),
        preferred_element_type=jnp.float32,
    )


def solution(mesh):
    return jax.shard_map(
        functools.partial(on_device, mesh.shape["store"]),
        mesh=mesh,
        in_specs=(
            P("groups", "store"),
            P("groups", "store"),
            P(),
            P(),
            P(),
            P(),
            P(("groups", "store"), None),
        ),
        out_specs=P("groups", "store"),
        check_vma=False,
    )
```

```python
import functools

import jax
import jax.numpy as jnp
from jax import lax
from jax.experimental import pallas as pl
from jax.experimental.pallas import tpu as pltpu
from jax.sharding import PartitionSpec as P

LEN = 4096
BLOCK = 32
LANES = 128
HALF = LANES // 2
SLOTS = 4
VMEM_LIMIT = 16 * 1024 * 1024

ANY = pl.BlockSpec(memory_space=pl.ANY)
IN_HBM = pl.BlockSpec(memory_space=pltpu.HBM)
IN_VMEM = pl.BlockSpec(memory_space=pltpu.VMEM)
IN_SMEM = pl.BlockSpec(memory_space=pltpu.SMEM)
PARAMS = pltpu.CompilerParams(vmem_limit_bytes=VMEM_LIMIT)


def build_in(first, index_ref, values_ref, w_ref, list_ref, acc_ref):
    groups, picks = index_ref.shape
    cwidth = values_ref.shape[1]
    count = acc_ref.shape[0]
    acc_ref[...] = jnp.zeros_like(acc_ref)
    found = jnp.int32(0)
    for c in range(groups):

        def scan(k, found, c=c):
            block = index_ref[c, k] - first
            list_ref[0, found] = c * picks + k
            list_ref[1, found] = block
            list_ref[2, found] = c * cwidth
            return found + jnp.where((block >= 0) & (block < count), 1, 0).astype(jnp.int32)

        found = lax.fori_loop(0, picks, scan, found, unroll=8)

    def add(i, carry):
        rows = pl.ds(pl.multiple_of(list_ref[2, i], cwidth), cwidth)
        acc_ref[list_ref[1, i], rows, :BLOCK] += values_ref[list_ref[0, i]].astype(jnp.float32)
        return carry

    lax.fori_loop(0, found, add, jnp.int32(0))
    for n in range(count):
        block = acc_ref[n]
        wide = jnp.concatenate([block, jnp.zeros_like(block)], axis=0).T[:BLOCK]
        rows = slice(n * BLOCK, (n + 1) * BLOCK)
        w_ref[0, rows] = wide.astype(jnp.bfloat16)
        w_ref[1, rows] = pltpu.roll(wide, HALF, 1).astype(jnp.bfloat16)


def build_out_kernel(count, first_ref, index_ref, values_ref, *rest):
    w_ref, by_block_ref, wide_ref = rest[-3:]
    groups, picks = index_ref.shape
    cwidth = values_ref.shape[1] // BLOCK
    ids = lax.broadcasted_iota(jnp.int32, (LANES, picks), 0) + first_ref[0]
    for c in range(groups):
        chosen = (index_ref[c : c + 1, :] == ids).astype(jnp.float32).astype(jnp.bfloat16)
        by_block_ref[c] = lax.dot_general(
            values_ref[c], chosen, (((1,), (1,)), ((), ())), preferred_element_type=jnp.float32
        )
    low = lax.broadcasted_iota(jnp.int32, (count, LANES), 1) < HALF
    for r in range(0, BLOCK, 2):
        rows = [
            by_block_ref[c, (r + odd) * cwidth : (r + odd + 1) * cwidth, :]
            for odd in (0, 1)
            for c in range(groups)
        ]
        pair = jnp.concatenate(rows, axis=0).T[:count]
        swapped = pltpu.roll(pair, HALF, 1)
        wide_ref[0, pl.ds(r, count, stride=BLOCK), :] = jnp.where(low, pair, 0.0)
        wide_ref[0, pl.ds(r + 1, count, stride=BLOCK), :] = jnp.where(low, swapped, 0.0)
        wide_ref[1, pl.ds(r, count, stride=BLOCK), :] = jnp.where(low, 0.0, swapped)
        wide_ref[1, pl.ds(r + 1, count, stride=BLOCK), :] = jnp.where(low, 0.0, pair)
    w_ref[...] = wide_ref[...].astype(jnp.bfloat16)


def build_out(index, values, first, count, after=()):
    groups, picks = index.shape
    values = values.transpose(0, 2, 3, 1).reshape(groups, -1, picks)
    rows = count * BLOCK
    return pl.pallas_call(
        functools.partial(build_out_kernel, count),
        out_shape=pltpu.VMEM((2, rows, LANES), jnp.bfloat16),
        in_specs=[IN_SMEM, IN_VMEM, IN_VMEM] + [ANY] * len(after),
        out_specs=IN_VMEM,
        scratch_shapes=[
            pltpu.VMEM((groups, values.shape[1], LANES), jnp.float32),
            pltpu.VMEM((2, rows, LANES), jnp.float32),
        ],
        compiler_params=PARAMS,
        cost_estimate=pl.CostEstimate(flops=10**9, bytes_accessed=values.size * 2, transcendentals=0),
    )(first[None].astype(jnp.int32), index, values, *after)


def project_kernel(tile, cuts, has_add, builds, after, through, *refs):
    refs = list(refs)
    roles_ref = refs.pop(0)
    x_hbm = refs.pop(0)
    if builds:
        index_hbm, values_hbm = refs.pop(0), refs.pop(0)
    else:
        w_ref = refs.pop(0)
    add_ref = refs.pop(0) if has_add else None
    refs = refs[after + through :]
    outs = [refs.pop(0) for _ in range(1 + max(cut[0] for cut in cuts))]
    if builds:
        w_ref = refs.pop(0)
    refs = refs[through:]
    buf, sems = refs.pop(0), refs.pop(0)
    steps, filled = [], [0] * len(outs)
    for array, role, start, rows in cuts:
        for at in range(0, rows, tile):
            steps.append((array, role, start + at, filled[array]))
            filled[array] += tile

    def copies(i):
        _, role, row, _ = steps[i]
        base = pl.multiple_of(roles_ref[role] * LEN + roles_ref[4] * (LEN // 4) + row, tile)
        slot = i % SLOTS
        return [
            pltpu.make_async_copy(
                x_hbm.at[pl.ds(base + side * (LEN // 2), tile), :], buf.at[slot, side], sems.at[slot, side]
            )
            for side in (0, 1)
        ]

    if builds:
        index_ref, values_ref, build_sems, list_ref, acc_ref = refs
        loads = [
            pltpu.make_async_copy(index_hbm, index_ref, build_sems.at[0]),
            pltpu.make_async_copy(values_hbm, values_ref, build_sems.at[1]),
        ]
        for load in loads:
            load.start()
    for i in range(min(SLOTS, len(steps))):
        for copy in copies(i):
            copy.start()
    if builds:
        for load in loads:
            load.wait()
        build_in(roles_ref[5], index_ref, values_ref, w_ref, list_ref, acc_ref)
    for i, (array, _, _, at) in enumerate(steps):
        for copy in copies(i):
            copy.wait()
        slot = i % SLOTS
        value = jnp.dot(buf[slot, 0], w_ref[0], preferred_element_type=jnp.float32)
        value += jnp.dot(buf[slot, 1], w_ref[1], preferred_element_type=jnp.float32)
        if has_add:
            value += add_ref[i * tile : (i + 1) * tile, :]
        outs[array][at : at + tile, :] = value
        if i + SLOTS < len(steps):
            for copy in copies(i + SLOTS):
                copy.start()


def project(x, w, roles, add, tile, cuts, after=(), through=()):
    depth = x.shape[1]
    x = pltpu.with_memory_space_constraint(x, pltpu.HBM)
    rows = sum(cut[3] for cut in cuts)
    builds = isinstance(w, tuple)
    out_shape = [
        pltpu.VMEM((sum(cut[3] for cut in cuts if cut[0] == array), LANES), jnp.float32)
        for array in range(1 + max(cut[0] for cut in cuts))
    ]
    scratch = [
        pltpu.VMEM((SLOTS, 2, tile, depth), x.dtype),
        pltpu.SemaphoreType.DMA((SLOTS, 2)),
    ]
    if builds:
        index, values, count = w
        groups, picks = index.shape
        cwidth = values.shape[3]
        values = values.transpose(0, 1, 3, 2).reshape(groups * picks, cwidth, BLOCK)
        index = pltpu.with_memory_space_constraint(index, pltpu.HBM)
        values = pltpu.with_memory_space_constraint(values, pltpu.HBM)
        args = [roles, x, index, values]
        in_specs = [IN_SMEM, IN_HBM, IN_HBM, IN_HBM]
        out_shape.append(pltpu.VMEM((2, count * BLOCK, LANES), jnp.bfloat16))
        scratch += [
            pltpu.SMEM(index.shape, index.dtype),
            pltpu.VMEM(values.shape, values.dtype),
            pltpu.SemaphoreType.DMA((2,)),
            pltpu.SMEM((3, groups * picks), jnp.int32),
            pltpu.VMEM((count, groups * cwidth, LANES), jnp.float32),
        ]
    else:
        args = [roles, x, w]
        in_specs = [IN_SMEM, IN_HBM, IN_VMEM]
    if add is not None:
        args.append(add)
        in_specs.append(IN_VMEM)
    return pl.pallas_call(
        functools.partial(project_kernel, tile, cuts, add is not None, builds, len(after), len(through)),
        out_shape=out_shape + [jax.ShapeDtypeStruct(t.shape, t.dtype) for t in through],
        in_specs=in_specs + [ANY] * (len(after) + len(through)),
        out_specs=[IN_VMEM] * len(out_shape) + [ANY] * len(through),
        input_output_aliases={
            len(args) + len(after) + i: len(out_shape) + i for i in range(len(through))
        },
        scratch_shapes=scratch,
        compiler_params=PARAMS,
        cost_estimate=pl.CostEstimate(
            flops=rows * depth * LANES, bytes_accessed=rows * depth, transcendentals=0
        ),
    )(*args, *after, *through)


def held(values, after):
    count = len(values)
    return pl.pallas_call(
        lambda *refs: None,
        out_shape=[jax.ShapeDtypeStruct(v.shape, v.dtype) for v in values],
        in_specs=[ANY] * (count + len(after)),
        out_specs=[ANY] * count,
        input_output_aliases={i: i for i in range(count)},
        cost_estimate=pl.CostEstimate(flops=0, bytes_accessed=0, transcendentals=0),
    )(*values, *after)


def contract(left, right):
    pair = lax.dot_general(
        left,
        right,
        (((0,), (0,)), ((), ())),
        precision=lax.Precision.HIGHEST,
        preferred_element_type=jnp.float32,
    )
    return pair[:HALF, :HALF] + pair[HALF:, HALF:]


def reduced_examples(tokens, up_grad, in_index, in_values, out_index, out_values):
    rank = lax.axis_index("store")
    core, x, z_low = rank % 2, (rank // 2) % 2, (rank // 4) % 2

    def swap(value, bit):
        return lax.ppermute(value, "store", [(i, i ^ bit) for i in range(16)])

    feat_blocks = tokens.shape[1] // BLOCK
    hidden_blocks = up_grad.shape[1] // BLOCK

    def roles(half):
        seqs = [1 - x, x, 3 - x, 2 + x]
        return jnp.stack([*seqs, half, rank * feat_blocks]).astype(jnp.int32)

    send, keep = roles(1 - core), roles(core)
    rows = LEN // 4
    half = rows // 2
    in_tile, out_tile = 256, 256

    def z_halves(value):
        halves = value.reshape(2, half, LANES)
        gone = lax.dynamic_index_in_dim(halves, 1 - z_low, 0, keepdims=False)
        kept = lax.dynamic_index_in_dim(halves, z_low, 0, keepdims=False)
        return kept, swap(gone, 4)

    def z_whole(kept):
        got = swap(kept, 4)
        return jnp.where(z_low == 0, jnp.stack([kept, got]), jnp.stack([got, kept])).reshape(-1, LANES)

    whole_a = [(0, 0, 0, rows), (1, 1, 0, rows)]
    whole_b = [(0, 2, 0, rows), (1, 3, 0, rows)]
    sent, in_w = project(
        tokens,
        (in_index, in_values, feat_blocks),
        send,
        None,
        in_tile,
        [(0, s, 0, rows) for s in range(4)],
    )
    got = swap(sent, 1)
    out_w = build_out(out_index, out_values, rank * hidden_blocks, hidden_blocks, after=(sent,))
    oa, in_a, ob, in_b = project(
        tokens, in_w, keep, got, in_tile, [(s, s, 0, rows) for s in range(4)], after=(out_w,)
    )
    got_in_a, got_in_b = swap(oa, 2), swap(ob, 2)
    sent_b, sent_a, in_a = project(
        up_grad,
        out_w,
        send,
        None,
        out_tile,
        [(0, 2, 0, rows), (0, 3, 0, rows), (1, 0, 0, rows), (1, 1, 0, rows)],
        after=(in_b,),
        through=(in_a,),
    )
    in_a = in_a + got_in_a
    sent_b, sent_a = held((sent_b, sent_a), (in_a,))
    got_b, got_a = swap(sent_b, 1), swap(sent_a, 1)
    in_a, got_in_a = z_halves(in_a)
    ob, out_b, in_a, in_b = project(
        up_grad, out_w, keep, got_b, out_tile, whole_b, after=(sent_a,), through=(in_a, in_b)
    )
    got_out_b = swap(ob, 2)
    in_a = in_a + got_in_a
    got_in_a = swap(in_a, 8)
    in_b, got_z_b = z_halves(in_b + got_in_b)
    oa, out_a, out_b, in_b = project(
        up_grad, out_w, keep, got_a, out_tile, whole_a, after=(in_a,), through=(out_b, in_b)
    )
    in_b = in_b + got_z_b
    (in_a,) = held((in_a + got_in_a,), (oa,))
    (oa,) = held((oa,), (in_b,))
    got_out_a = swap(oa, 2)
    in_a = z_whole(in_a)
    in_b = in_b + swap(in_b, 8)
    out_b, got_out_b = z_halves(out_b + got_out_b)
    out_b = out_b + got_out_b
    out_a = out_a + got_out_a
    example = jnp.stack([contract(in_a, out_a), contract(in_b, out_b)]).reshape(-1, LANES)
    example = example + swap(example, 1)
    example = example + swap(example, 4) + swap(example, 8) + swap(example, 12)
    other = swap(example, 2)
    example, other = example.reshape(2, HALF * HALF), other.reshape(2, HALF * HALF)
    first = jnp.where(x == 0, example, other)
    second = jnp.where(x == 0, other, example)
    return jnp.stack([first, second], axis=1).reshape(4, HALF * HALF) / LEN


def summed_examples(tokens, up_grad, in_index, in_values, out_index, out_values):
    rank = lax.axis_index("store")
    seqs = tokens.shape[0] // LEN
    feat_blocks = tokens.shape[1] // BLOCK
    hidden_blocks = up_grad.shape[1] // BLOCK
    out_proj = build_out(out_index, out_values, rank * hidden_blocks, hidden_blocks)
    rows = LEN // 4

    def packed(kind, w):
        made = []
        for s in range(0, seqs, 2):
            for h in (0, 1):
                roles = jnp.stack([s, s + 1, s, s, h, rank * feat_blocks]).astype(jnp.int32)
                first, second, *rest = project(
                    kind, w, roles, None, 256, [(0, 0, 0, rows), (1, 1, 0, rows)]
                )
                if rest:
                    w = rest[0]
                made.append(jnp.stack([first, second]))
        return jnp.concatenate(made)

    ins, outs = lax.psum(
        (packed(tokens, (in_index, in_values, feat_blocks)), packed(up_grad, out_proj)), "store"
    )
    pair = jnp.einsum("slp,slq->spq", ins, outs, precision=lax.Precision.HIGHEST)
    pair = pair[:, :HALF, :HALF] + pair[:, HALF:, HALF:]
    pair = pair.reshape(seqs // 2, 2, 2, HALF * HALF).sum(1) / LEN
    return pair.reshape(seqs, HALF * HALF)


def on_device(size, tokens, up_grad, in_index, in_values, out_index, out_values, stored):
    whole = reduced_examples if size == 16 and tokens.shape[0] == 4 * LEN else summed_examples
    example = whole(tokens, up_grad, in_index, in_values, out_index, out_values)
    return lax.dot_general(
        example.astype(jnp.bfloat16),
        stored,
        (((1,), (1,)), ((), ())),
        preferred_element_type=jnp.float32,
    )


def solution(mesh):
    return jax.shard_map(
        functools.partial(on_device, mesh.shape["store"]),
        mesh=mesh,
        in_specs=(
            P("groups", "store"),
            P("groups", "store"),
            P(),
            P(),
            P(),
            P(),
            P(("groups", "store"), None),
        ),
        out_specs=P("groups", "store"),
        check_vma=False,
    )
```

```python
import functools

import jax
import jax.numpy as jnp
from jax import lax
from jax.experimental import pallas as pl
from jax.experimental.pallas import tpu as pltpu
from jax.sharding import PartitionSpec as P

LEN = 4096
BLOCK = 32
LANES = 128
HALF = LANES // 2
SLOTS = 4
VMEM_LIMIT = 12 * 1024 * 1024

ANY = pl.BlockSpec(memory_space=pl.ANY)
IN_HBM = pl.BlockSpec(memory_space=pltpu.HBM)
IN_VMEM = pl.BlockSpec(memory_space=pltpu.VMEM)
IN_SMEM = pl.BlockSpec(memory_space=pltpu.SMEM)
PARAMS = pltpu.CompilerParams(vmem_limit_bytes=VMEM_LIMIT)


def build_in(first, index_ref, values_ref, w_ref, list_ref, acc_ref):
    groups, picks = index_ref.shape
    cwidth = values_ref.shape[1]
    count = acc_ref.shape[0]
    acc_ref[...] = jnp.zeros_like(acc_ref)
    found = jnp.int32(0)
    for c in range(groups):

        def scan(k, found, c=c):
            block = index_ref[c, k] - first
            list_ref[0, found] = c * picks + k
            list_ref[1, found] = block
            list_ref[2, found] = c * cwidth
            return found + jnp.where((block >= 0) & (block < count), 1, 0).astype(jnp.int32)

        found = lax.fori_loop(0, picks, scan, found, unroll=8)

    def add(i, carry):
        rows = pl.ds(pl.multiple_of(list_ref[2, i], cwidth), cwidth)
        acc_ref[list_ref[1, i], rows, :BLOCK] += values_ref[list_ref[0, i]].astype(jnp.float32)
        return carry

    lax.fori_loop(0, found, add, jnp.int32(0))
    for n in range(count):
        block = acc_ref[n]
        wide = jnp.concatenate([block, jnp.zeros_like(block)], axis=0).T[:BLOCK]
        rows = slice(n * BLOCK, (n + 1) * BLOCK)
        w_ref[0, rows] = wide.astype(jnp.bfloat16)
        w_ref[1, rows] = pltpu.roll(wide, HALF, 1).astype(jnp.bfloat16)


def build_out_kernel(count, first_ref, index_ref, values_ref, *rest):
    w_ref, by_block_ref, wide_ref = rest[-3:]
    groups, picks = index_ref.shape
    cwidth = values_ref.shape[1] // BLOCK
    ids = lax.broadcasted_iota(jnp.int32, (LANES, picks), 0) + first_ref[0]
    for c in range(groups):
        chosen = (index_ref[c : c + 1, :] == ids).astype(jnp.float32).astype(jnp.bfloat16)
        by_block_ref[c] = lax.dot_general(
            values_ref[c], chosen, (((1,), (1,)), ((), ())), preferred_element_type=jnp.float32
        )
    low = lax.broadcasted_iota(jnp.int32, (count, LANES), 1) < HALF
    for r in range(0, BLOCK, 2):
        rows = [
            by_block_ref[c, (r + odd) * cwidth : (r + odd + 1) * cwidth, :]
            for odd in (0, 1)
            for c in range(groups)
        ]
        pair = jnp.concatenate(rows, axis=0).T[:count]
        swapped = pltpu.roll(pair, HALF, 1)
        wide_ref[0, pl.ds(r, count, stride=BLOCK), :] = jnp.where(low, pair, 0.0)
        wide_ref[0, pl.ds(r + 1, count, stride=BLOCK), :] = jnp.where(low, swapped, 0.0)
        wide_ref[1, pl.ds(r, count, stride=BLOCK), :] = jnp.where(low, 0.0, swapped)
        wide_ref[1, pl.ds(r + 1, count, stride=BLOCK), :] = jnp.where(low, 0.0, pair)
    w_ref[...] = wide_ref[...].astype(jnp.bfloat16)


def build_out(index, values, first, count, after=()):
    groups, picks = index.shape
    values = values.transpose(0, 2, 3, 1).reshape(groups, -1, picks)
    rows = count * BLOCK
    return pl.pallas_call(
        functools.partial(build_out_kernel, count),
        out_shape=pltpu.VMEM((2, rows, LANES), jnp.bfloat16),
        in_specs=[IN_SMEM, IN_VMEM, IN_VMEM] + [ANY] * len(after),
        out_specs=IN_VMEM,
        scratch_shapes=[
            pltpu.VMEM((groups, values.shape[1], LANES), jnp.float32),
            pltpu.VMEM((2, rows, LANES), jnp.float32),
        ],
        compiler_params=PARAMS,
        cost_estimate=pl.CostEstimate(flops=10**9, bytes_accessed=values.size * 2, transcendentals=0),
    )(first[None].astype(jnp.int32), index, values, *after)


def project_kernel(tile, cuts, has_add, builds, after, through, *refs):
    refs = list(refs)
    roles_ref = refs.pop(0)
    x_hbm = refs.pop(0)
    if builds:
        index_hbm, values_hbm = refs.pop(0), refs.pop(0)
    else:
        w_ref = refs.pop(0)
    add_ref = refs.pop(0) if has_add else None
    refs = refs[after + through :]
    outs = [refs.pop(0) for _ in range(1 + max(cut[0] for cut in cuts))]
    if builds:
        w_ref = refs.pop(0)
    refs = refs[through:]
    buf, sems = refs.pop(0), refs.pop(0)
    steps, filled = [], [0] * len(outs)
    for array, role, start, rows in cuts:
        for at in range(0, rows, tile):
            steps.append((array, role, start + at, filled[array]))
            filled[array] += tile

    def copies(i):
        _, role, row, _ = steps[i]
        base = pl.multiple_of(roles_ref[role] * LEN + roles_ref[4] * (LEN // 4) + row, tile)
        slot = i % SLOTS
        return [
            pltpu.make_async_copy(
                x_hbm.at[pl.ds(base + side * (LEN // 2), tile), :], buf.at[slot, side], sems.at[slot, side]
            )
            for side in (0, 1)
        ]

    if builds:
        index_ref, values_ref, build_sems, list_ref, acc_ref = refs
        loads = [
            pltpu.make_async_copy(index_hbm, index_ref, build_sems.at[0]),
            pltpu.make_async_copy(values_hbm, values_ref, build_sems.at[1]),
        ]
        for load in loads:
            load.start()
    for i in range(min(SLOTS, len(steps))):
        for copy in copies(i):
            copy.start()
    if builds:
        for load in loads:
            load.wait()
        build_in(roles_ref[5], index_ref, values_ref, w_ref, list_ref, acc_ref)
    for i, (array, _, _, at) in enumerate(steps):
        for copy in copies(i):
            copy.wait()
        slot = i % SLOTS
        value = jnp.dot(buf[slot, 0], w_ref[0], preferred_element_type=jnp.float32)
        value += jnp.dot(buf[slot, 1], w_ref[1], preferred_element_type=jnp.float32)
        if has_add:
            value += add_ref[i * tile : (i + 1) * tile, :]
        outs[array][at : at + tile, :] = value
        if i + SLOTS < len(steps):
            for copy in copies(i + SLOTS):
                copy.start()


def project(x, w, roles, add, tile, cuts, after=(), through=()):
    depth = x.shape[1]
    x = pltpu.with_memory_space_constraint(x, pltpu.HBM)
    rows = sum(cut[3] for cut in cuts)
    builds = isinstance(w, tuple)
    out_shape = [
        pltpu.VMEM((sum(cut[3] for cut in cuts if cut[0] == array), LANES), jnp.float32)
        for array in range(1 + max(cut[0] for cut in cuts))
    ]
    scratch = [
        pltpu.VMEM((SLOTS, 2, tile, depth), x.dtype),
        pltpu.SemaphoreType.DMA((SLOTS, 2)),
    ]
    if builds:
        index, values, count = w
        groups, picks = index.shape
        cwidth = values.shape[3]
        values = values.transpose(0, 1, 3, 2).reshape(groups * picks, cwidth, BLOCK)
        index = pltpu.with_memory_space_constraint(index, pltpu.HBM)
        values = pltpu.with_memory_space_constraint(values, pltpu.HBM)
        args = [roles, x, index, values]
        in_specs = [IN_SMEM, IN_HBM, IN_HBM, IN_HBM]
        out_shape.append(pltpu.VMEM((2, count * BLOCK, LANES), jnp.bfloat16))
        scratch += [
            pltpu.SMEM(index.shape, index.dtype),
            pltpu.VMEM(values.shape, values.dtype),
            pltpu.SemaphoreType.DMA((2,)),
            pltpu.SMEM((3, groups * picks), jnp.int32),
            pltpu.VMEM((count, groups * cwidth, LANES), jnp.float32),
        ]
    else:
        args = [roles, x, w]
        in_specs = [IN_SMEM, IN_HBM, IN_VMEM]
    if add is not None:
        args.append(add)
        in_specs.append(IN_VMEM)
    return pl.pallas_call(
        functools.partial(project_kernel, tile, cuts, add is not None, builds, len(after), len(through)),
        out_shape=out_shape + [jax.ShapeDtypeStruct(t.shape, t.dtype) for t in through],
        in_specs=in_specs + [ANY] * (len(after) + len(through)),
        out_specs=[IN_VMEM] * len(out_shape) + [ANY] * len(through),
        input_output_aliases={
            len(args) + len(after) + i: len(out_shape) + i for i in range(len(through))
        },
        scratch_shapes=scratch,
        compiler_params=PARAMS,
        cost_estimate=pl.CostEstimate(
            flops=rows * depth * LANES, bytes_accessed=rows * depth, transcendentals=0
        ),
    )(*args, *after, *through)


def held(values, after):
    count = len(values)
    return pl.pallas_call(
        lambda *refs: None,
        out_shape=[jax.ShapeDtypeStruct(v.shape, v.dtype) for v in values],
        in_specs=[ANY] * (count + len(after)),
        out_specs=[ANY] * count,
        input_output_aliases={i: i for i in range(count)},
        cost_estimate=pl.CostEstimate(flops=0, bytes_accessed=0, transcendentals=0),
    )(*values, *after)


def contract(left, right):
    pair = lax.dot_general(
        left,
        right,
        (((0,), (0,)), ((), ())),
        precision=lax.Precision.HIGHEST,
        preferred_element_type=jnp.float32,
    )
    return pair[:HALF, :HALF] + pair[HALF:, HALF:]


def reduced_examples(tokens, up_grad, in_index, in_values, out_index, out_values):
    rank = lax.axis_index("store")
    core, x, z_low = rank % 2, (rank // 2) % 2, (rank // 4) % 2

    def swap(value, bit):
        return lax.ppermute(value, "store", [(i, i ^ bit) for i in range(16)])

    feat_blocks = tokens.shape[1] // BLOCK
    hidden_blocks = up_grad.shape[1] // BLOCK

    def roles(half):
        seqs = [1 - x, x, 3 - x, 2 + x]
        return jnp.stack([*seqs, half, rank * feat_blocks]).astype(jnp.int32)

    send, keep = roles(1 - core), roles(core)
    rows = LEN // 4
    half = rows // 2
    in_tile, out_tile = 256, 256

    def z_halves(value):
        halves = value.reshape(2, half, LANES)
        gone = lax.dynamic_index_in_dim(halves, 1 - z_low, 0, keepdims=False)
        kept = lax.dynamic_index_in_dim(halves, z_low, 0, keepdims=False)
        return kept, swap(gone, 4)

    def z_whole(kept):
        got = swap(kept, 4)
        return jnp.where(z_low == 0, jnp.stack([kept, got]), jnp.stack([got, kept])).reshape(-1, LANES)

    whole_a = [(0, 0, 0, rows), (1, 1, 0, rows)]
    whole_b = [(0, 2, 0, rows), (1, 3, 0, rows)]
    sent, in_w = project(
        tokens,
        (in_index, in_values, feat_blocks),
        send,
        None,
        in_tile,
        [(0, s, 0, rows) for s in range(4)],
    )
    got = swap(sent, 1)
    out_w = build_out(out_index, out_values, rank * hidden_blocks, hidden_blocks, after=(sent,))
    oa, in_a, ob, in_b = project(
        tokens, in_w, keep, got, in_tile, [(s, s, 0, rows) for s in range(4)], after=(out_w,)
    )
    got_in_a, got_in_b = swap(oa, 2), swap(ob, 2)
    sent_b, sent_a, in_a = project(
        up_grad,
        out_w,
        send,
        None,
        out_tile,
        [(0, 2, 0, rows), (0, 3, 0, rows), (1, 0, 0, rows), (1, 1, 0, rows)],
        after=(in_b,),
        through=(in_a,),
    )
    in_a = in_a + got_in_a
    sent_b, sent_a = held((sent_b, sent_a), (in_a,))
    got_b, got_a = swap(sent_b, 1), swap(sent_a, 1)
    in_a, got_in_a = z_halves(in_a)
    ob, out_b, in_a, in_b = project(
        up_grad, out_w, keep, got_b, out_tile, whole_b, after=(sent_a,), through=(in_a, in_b)
    )
    got_out_b = swap(ob, 2)
    in_a = in_a + got_in_a
    got_in_a = swap(in_a, 8)
    in_b, got_z_b = z_halves(in_b + got_in_b)
    oa, out_a, out_b, in_b = project(
        up_grad, out_w, keep, got_a, out_tile, whole_a, after=(in_a,), through=(out_b, in_b)
    )
    in_b = in_b + got_z_b
    (in_a,) = held((in_a + got_in_a,), (oa,))
    (oa,) = held((oa,), (in_b,))
    got_out_a = swap(oa, 2)
    in_a = z_whole(in_a)
    in_b = in_b + swap(in_b, 8)
    out_b, got_out_b = z_halves(out_b + got_out_b)
    out_b = out_b + got_out_b
    out_a = out_a + got_out_a
    example = jnp.stack([contract(in_a, out_a), contract(in_b, out_b)]).reshape(-1, LANES)
    example = example + swap(example, 1)
    example = example + swap(example, 4) + swap(example, 8) + swap(example, 12)
    other = swap(example, 2)
    example, other = example.reshape(2, HALF * HALF), other.reshape(2, HALF * HALF)
    first = jnp.where(x == 0, example, other)
    second = jnp.where(x == 0, other, example)
    return jnp.stack([first, second], axis=1).reshape(4, HALF * HALF) / LEN


def summed_examples(tokens, up_grad, in_index, in_values, out_index, out_values):
    rank = lax.axis_index("store")
    seqs = tokens.shape[0] // LEN
    feat_blocks = tokens.shape[1] // BLOCK
    hidden_blocks = up_grad.shape[1] // BLOCK
    out_proj = build_out(out_index, out_values, rank * hidden_blocks, hidden_blocks)
    rows = LEN // 4

    def packed(kind, w):
        made = []
        for s in range(0, seqs, 2):
            for h in (0, 1):
                roles = jnp.stack([s, s + 1, s, s, h, rank * feat_blocks]).astype(jnp.int32)
                first, second, *rest = project(
                    kind, w, roles, None, 256, [(0, 0, 0, rows), (1, 1, 0, rows)]
                )
                if rest:
                    w = rest[0]
                made.append(jnp.stack([first, second]))
        return jnp.concatenate(made)

    ins, outs = lax.psum(
        (packed(tokens, (in_index, in_values, feat_blocks)), packed(up_grad, out_proj)), "store"
    )
    pair = jnp.einsum("slp,slq->spq", ins, outs, precision=lax.Precision.HIGHEST)
    pair = pair[:, :HALF, :HALF] + pair[:, HALF:, HALF:]
    pair = pair.reshape(seqs // 2, 2, 2, HALF * HALF).sum(1) / LEN
    return pair.reshape(seqs, HALF * HALF)


def on_device(size, tokens, up_grad, in_index, in_values, out_index, out_values, stored):
    whole = reduced_examples if size == 16 and tokens.shape[0] == 4 * LEN else summed_examples
    example = whole(tokens, up_grad, in_index, in_values, out_index, out_values)
    return lax.dot_general(
        example.astype(jnp.bfloat16),
        stored,
        (((1,), (1,)), ((), ())),
        preferred_element_type=jnp.float32,
    )


def solution(mesh):
    return jax.shard_map(
        functools.partial(on_device, mesh.shape["store"]),
        mesh=mesh,
        in_specs=(
            P("groups", "store"),
            P("groups", "store"),
            P(),
            P(),
            P(),
            P(),
            P(("groups", "store"), None),
        ),
        out_specs=P("groups", "store"),
        check_vma=False,
    )
```
